256 devices in a mesh: gx: 8 (over x, core), gy: 8 (over z_hi, y), pa: 4 (over z_lo).
Axes of the slice: x: 4, y: 4, z: 8 (z_hi: 2, z_lo: 4; z = z_hi * 4 + z_lo), core: 2. Of those that a mesh axis runs over, the one named last changes fastest.
Arguments:
- mixing_ratios: float32 [120, 1, 32, 1024], P(None, None, 'gx', 'gy'), may hold values from 0.1 to 2
- derivative_field: float32 [120, 16, 1, 32, 1024], P(None, 'pa', None, 'gx', 'gy'), may hold values from -6 to 6
- thermal_kelvin: float32 [1, 32, 1024], P(None, 'gx', 'gy'), may hold values from 260 to 310
- eastward_cfl_ratio: float32 [1, 32, 1024], P(None, 'gx', 'gy'), may hold values from -0.3 to 0.3
- northward_cfl_ratio: float32 [1, 32, 1024], P(None, 'gx', 'gy'), may hold values from -0.3 to 0.3
- lateral_mixing_coef: float32 [1, 32, 1024], P(None, 'gx', 'gy'), may hold values from 0.02 to 0.08
- prefactor_times_dt: float32 [360], replicated, may hold values from 0.01 to 0.1
- barrier_kelvin: float32 [360], replicated, may hold values from 0 to 2000
- input_compound_pair: int32 [360, 2], replicated, may hold values from 0 to 119
- output_yield_matrix: int32 [120, 360], replicated, may hold values from 0 to 2
- partition_solver_matrices: bfloat16 [120, 120, 1, 32, 1024], P(None, None, None, ('gx', 'pa'), 'gy'), may hold values from -2 to 2
- ground_flux_per_tick: float32 [32, 1024], P('gx', 'gy'), may hold values from 0.5 to 2
- cell_zone_label: int32 [32, 1024], P('gx', 'gy'), may hold values from 0 to 7
- knob_target_compound: int32 [16], P('pa'), may hold values from 0 to 119
- knob_zone: int32 [16], P('pa'), may hold values from 0 to 7
Outputs:
- new_sens: float32 [120, 16, 1, 32, 1024], P(None, 'pa', None, 'gx', 'gy')
The draws below stay inside these ranges and needn't reach their ends.
All inputs are finite; a program needn't handle non-finite values.
Results may differ from the reference program's by a relative error of at most 0.0021.
Values may be sent and summed in bfloat16 or wider, within the bound.
A program may use at most 128 MiB of HBM per device.

```python
import math
import jax
import jax.numpy as jnp
from jax import lax

S = 120
R = 360
P_SIZE = 16
HEIGHT_LAYERS = 1
NSUB = 2
NREG = 8
GRID_EASTWARD = 32
GRID_NORTHWARD = 1024


def draw_partition_solver_matrices(key, part):
    array_shape = (S, S, HEIGHT_LAYERS, GRID_EASTWARD, GRID_NORTHWARD)
    spread = jnp.clip(jax.random.normal(key, array_shape, jnp.float32), -3.0, 3.0)
    diagonal_mask = lax.broadcasted_iota(jnp.int32, array_shape, 0) == lax.broadcasted_iota(jnp.int32, array_shape, 1)
    values = jnp.where(diagonal_mask, 1.0 + 0.2 * spread, spread * (0.5 * S ** (-0.5)))
    return values.astype(jnp.bfloat16)


def draw_output_yield_matrix(key, part):
    first_key, second_key, third_key = jax.random.split(key, 3)
    main_product = jax.random.randint(first_key, (R,), 0, S)
    main_yield = jax.random.randint(second_key, (R,), 1, 3)
    extra_roll = jax.random.randint(third_key, (S, R), 0, 100)
    species_ids = lax.broadcasted_iota(jnp.int32, (S, R), 0)
    yields = jnp.where(species_ids == main_product[None, :], main_yield[None, :], 0) + (extra_roll < 2).astype(jnp.int32)
    return jnp.minimum(yields, 2).astype(jnp.int32)


def with_ends(drawn, own_key, low, largest):
    longest = drawn.shape.index(max(drawn.shape))
    spots = []
    for shift in (0, 1):
        where = [jax.random.randint(jax.random.fold_in(own_key, axis), (), 0, length) for axis, length in enumerate(drawn.shape)]
        where[longest] = (where[longest] + shift) % drawn.shape[longest]
        spots.append(tuple(where))
    return drawn.at[spots[0]].set(low).at[spots[1]].set(largest)


def block_levels(rng, dims, cuts, least, largest):
    factor_of, own = 1.0, jax.random.fold_in(rng, 6)
    for axis_at, blocks in cuts:
        steps = jnp.exp(jax.random.uniform(jax.random.fold_in(own, axis_at), (blocks,), jnp.float32, least / len(cuts), largest / len(cuts)))
        factor_of = factor_of * jnp.repeat(steps, dims[axis_at] // blocks).reshape([-1 if axis == axis_at else 1 for axis in range(len(dims))])
    return factor_of


def centred(key, shape, scale, most, cuts=(), held_as=jnp.bfloat16):
    entries = jax.random.normal(key, shape, jnp.float32) * scale
    if len(cuts) > 0:
        entries = block_levels(key, shape, cuts, -0.22, 0.18) * entries
    return jnp.clip(entries, min=-most, max=most).astype(held_as)


def setup_inputs(seed: int = 0) -> dict:
    key_list = jax.random.split(jax.random.key(seed), 16)
    mixing_ratios = jnp.clip(jnp.exp(math.log(2.0) - 2.9957323 * jax.random.uniform(key_list[0], (S, HEIGHT_LAYERS, GRID_EASTWARD, GRID_NORTHWARD), jnp.float32) ** block_levels(key_list[0], (S, HEIGHT_LAYERS, GRID_EASTWARD, GRID_NORTHWARD), ((2, 8), (3, 8)), -0.2, 0.2)), 0.1, 2.0)
    derivative_field = centred(key_list[1], (S, P_SIZE, HEIGHT_LAYERS, GRID_EASTWARD, GRID_NORTHWARD), 1.0, 6.0, ((1, 4), (3, 8), (4, 8)), jnp.float32)
    thermal_kelvin = jnp.clip(260.0 + 50.0 * jax.random.uniform(key_list[2], (HEIGHT_LAYERS, GRID_EASTWARD, GRID_NORTHWARD), jnp.float32) ** block_levels(key_list[2], (HEIGHT_LAYERS, GRID_EASTWARD, GRID_NORTHWARD), ((1, 8), (2, 8)), -0.2, 0.2), 260.0, 310.0)
    eastward_cfl_ratio = jnp.clip(jax.random.uniform(key_list[3], (HEIGHT_LAYERS, GRID_EASTWARD, GRID_NORTHWARD), jnp.float32, -0.3, 0.3) * block_levels(key_list[3], (HEIGHT_LAYERS, GRID_EASTWARD, GRID_NORTHWARD), ((1, 8), (2, 8)), -0.4, 0.0), -0.3, 0.3)
    northward_cfl_ratio = jnp.clip(jax.random.uniform(key_list[4], (HEIGHT_LAYERS, GRID_EASTWARD, GRID_NORTHWARD), jnp.float32, -0.3, 0.3) * block_levels(key_list[4], (HEIGHT_LAYERS, GRID_EASTWARD, GRID_NORTHWARD), ((1, 8), (2, 8)), -0.4, 0.0), -0.3, 0.3)
    lateral_mixing_coef = jnp.clip(0.02 + 0.06 * jax.random.uniform(key_list[5], (HEIGHT_LAYERS, GRID_EASTWARD, GRID_NORTHWARD), jnp.float32) ** block_levels(key_list[5], (HEIGHT_LAYERS, GRID_EASTWARD, GRID_NORTHWARD), ((1, 8), (2, 8)), -0.2, 0.2), 0.02, 0.08)
    prefactor_times_dt = jnp.clip(jnp.exp(jax.random.uniform(key_list[6], (R,), jnp.float32, math.log(0.01), math.log(0.1))), 0.01, 0.1)
    barrier_kelvin = jnp.clip(jax.random.uniform(key_list[7], (R,), jnp.float32, 0.0, 2000.0), 0.0, 2000.0)
    input_compound_pair = with_ends(jax.random.randint(key_list[8], (R, 2), 0, S), jax.random.fold_in(key_list[8], 1), 0, S - 1).astype(jnp.int32)
    output_yield_matrix = draw_output_yield_matrix(jax.random.fold_in(key_list[15], 71), 0)
    partition_solver_matrices = draw_partition_solver_matrices(jax.random.fold_in(key_list[15], 71), 0)
    ground_flux_per_tick = jnp.clip(jnp.exp(math.log(2.0) - 1.3862944 * jax.random.uniform(key_list[11], (GRID_EASTWARD, GRID_NORTHWARD), jnp.float32) ** block_levels(key_list[11], (GRID_EASTWARD, GRID_NORTHWARD), ((0, 8), (1, 8)), -0.2, 0.2)), 0.5, 2.0)
    cell_zone_label = with_ends(jax.random.randint(key_list[12], (GRID_EASTWARD, GRID_NORTHWARD), 0, NREG), jax.random.fold_in(key_list[12], 1), 0, NREG - 1).astype(jnp.int32)
    knob_target_compound = with_ends(jax.random.randint(key_list[13], (P_SIZE,), 0, S), jax.random.fold_in(key_list[13], 1), 0, S - 1).astype(jnp.int32)
    knob_zone = with_ends(jax.random.randint(key_list[14], (P_SIZE,), 0, NREG), jax.random.fold_in(key_list[14], 1), 0, NREG - 1).astype(jnp.int32)
    return {"mixing_ratios": mixing_ratios, "derivative_field": derivative_field, "thermal_kelvin": thermal_kelvin, "eastward_cfl_ratio": eastward_cfl_ratio, "northward_cfl_ratio": northward_cfl_ratio, "lateral_mixing_coef": lateral_mixing_coef, "prefactor_times_dt": prefactor_times_dt, "barrier_kelvin": barrier_kelvin, "input_compound_pair": input_compound_pair, "output_yield_matrix": output_yield_matrix, "partition_solver_matrices": partition_solver_matrices, "ground_flux_per_tick": ground_flux_per_tick, "cell_zone_label": cell_zone_label, "knob_target_compound": knob_target_compound, "knob_zone": knob_zone}


def transport(fields, eastward_cfl_ratio, northward_cfl_ratio, lateral_mixing_coef):
    pad_spec = [(0, 0)] * (fields.ndim - 2) + [(1, 1), (1, 1)]
    for substep in range(NSUB):
        padded = jnp.pad(fields, pad_spec)
        center = padded[..., 1:-1, 1:-1]
        x_minus = padded[..., :-2, 1:-1]
        x_plus = padded[..., 2:, 1:-1]
        y_minus = padded[..., 1:-1, :-2]
        y_plus = padded[..., 1:-1, 2:]
        along_x = jnp.maximum(eastward_cfl_ratio, 0.0) * (center - x_minus) + jnp.minimum(eastward_cfl_ratio, 0.0) * (x_plus - center)
        along_y = jnp.maximum(northward_cfl_ratio, 0.0) * (center - y_minus) + jnp.minimum(northward_cfl_ratio, 0.0) * (y_plus - center)
        fields = center - along_x - along_y + lateral_mixing_coef * (x_plus + x_minus + y_plus + y_minus - 4.0 * center)
    return fields


def coefficients(conc_rows, scratch_lines, prefactor_times_dt, barrier_kelvin, input_compound_pair):
    rate_const = prefactor_times_dt[:, None, None, None] * jnp.exp(-barrier_kelvin[:, None, None, None] * (1.0 / scratch_lines[None] - 1.0 / 298.0))
    first_coef = rate_const * jnp.take(conc_rows, input_compound_pair[:, 1], axis=0)
    second = rate_const * jnp.take(conc_rows, input_compound_pair[:, 0], axis=0)
    return jnp.stack([first_coef, second]).astype(jnp.bfloat16)


def net_matrix(output_yield_matrix, input_compound_pair):
    species_ids = jnp.arange(output_yield_matrix.shape[0], dtype=jnp.int32)[:, None]
    consumed = (species_ids == input_compound_pair[None, :, 0]).astype(jnp.int32) + (species_ids == input_compound_pair[None, :, 1]).astype(jnp.int32)
    return (output_yield_matrix - consumed).astype(jnp.bfloat16)


def emission_source(species, levels, knob_target_compound, knob_zone, zone_rows, base_rows):
    hit_species = (jnp.arange(species, dtype=jnp.int32)[:, None] == knob_target_compound[None, :]).astype(jnp.float32)
    hit_zone = (zone_rows[None] == knob_zone[:, None, None]).astype(jnp.float32)
    surface = (jnp.arange(levels, dtype=jnp.int32) == 0).astype(jnp.float32)
    return hit_species[:, :, None, None, None] * hit_zone[None, :, None] * surface[None, None, :, None, None] * base_rows[None, None, None]


def apply_jacobian(tangent, coeffs, net_stoich, input_compound_pair):
    left_sens = jnp.take(tangent, input_compound_pair[:, 0], axis=0)
    right_sens = jnp.take(tangent, input_compound_pair[:, 1], axis=0)
    flux_bf = (coeffs[0][:, None] * left_sens + coeffs[1][:, None] * right_sens).astype(jnp.bfloat16)
    reaction_count = flux_bf.shape[0]
    product = jnp.dot(net_stoich, flux_bf.reshape(reaction_count, -1), preferred_element_type=jnp.float32)
    return product.reshape(tangent.shape)


def invert(blocks, rhs_bf):
    return jnp.einsum("ijlxy,jplxy->iplxy", blocks.astype(jnp.float32), rhs_bf.astype(jnp.float32))


def reference(mixing_ratios, derivative_field, thermal_kelvin, eastward_cfl_ratio, northward_cfl_ratio, lateral_mixing_coef, prefactor_times_dt, barrier_kelvin, input_compound_pair, output_yield_matrix, partition_solver_matrices, ground_flux_per_tick, cell_zone_label, knob_target_compound, knob_zone):
    moved_conc = transport(mixing_ratios, eastward_cfl_ratio, northward_cfl_ratio, lateral_mixing_coef)
    moved_sens = lax.map(lambda single: transport(single, eastward_cfl_ratio, northward_cfl_ratio, lateral_mixing_coef), derivative_field)
    net_stoich = net_matrix(output_yield_matrix, input_compound_pair)

    def one_row(eastward_position):
        conc_rows = lax.dynamic_slice_in_dim(moved_conc, eastward_position, 1, 2)
        scratch_lines = lax.dynamic_slice_in_dim(thermal_kelvin, eastward_position, 1, 1)
        tangent = lax.dynamic_slice_in_dim(moved_sens, eastward_position, 1, 3)
        blocks = lax.dynamic_slice_in_dim(partition_solver_matrices, eastward_position, 1, 3)
        base_rows = lax.dynamic_slice_in_dim(ground_flux_per_tick, eastward_position, 1, 0)
        zone_rows = lax.dynamic_slice_in_dim(cell_zone_label, eastward_position, 1, 0)
        coeffs = coefficients(conc_rows, scratch_lines, prefactor_times_dt, barrier_kelvin, input_compound_pair)
        source = emission_source(S, HEIGHT_LAYERS, knob_target_compound, knob_zone, zone_rows, base_rows)
        rhs_one = (apply_jacobian(tangent, coeffs, net_stoich, input_compound_pair) + source).astype(jnp.bfloat16)
        k_one = invert(blocks, rhs_one)
        rhs_two = (apply_jacobian(tangent + k_one, coeffs, net_stoich, input_compound_pair) + source - 2.0 * k_one).astype(jnp.bfloat16)
        k_two = invert(blocks, rhs_two)
        return (tangent + 1.5 * k_one + 0.5 * k_two)[:, :, :, 0, :]

    stacked = lax.map(one_row, jnp.arange(GRID_EASTWARD, dtype=jnp.int32))
    return jnp.transpose(stacked, (1, 2, 3, 0, 4))
```

```python
import functools

import jax
import jax.numpy as jnp
from jax import lax
from jax.experimental import pallas as pl
from jax.experimental.pallas import tpu as pltpu
from jax.sharding import PartitionSpec as P

NSUB = 2
LANES = 128
F32 = jnp.float32
BF16 = jnp.bfloat16
MESH = pl.DeviceIdType.MESH


def contract(a, b, dims):
    return lax.dot_general(a, b, (dims, ((), ())), preferred_element_type=F32)


def kernel(
    dims,
    sens_hbm,
    conc_hbm,
    blocks_hbm,
    temp_ref,
    u_ref,
    v_ref,
    mix_ref,
    ground_ref,
    zone_ref,
    knob_ref,
    rate_ref,
    pick_ref,
    net_ref,
    out_ref,
    sens_in,
    conc_in,
    blocks_in,
    solver,
    fields,
    stepped,
    weights,
    xs_send,
    xs_recv,
    ys_send,
    ys_recv,
    fwd_send,
    fwd_recv,
    ret_send,
    ret_recv,
    knobs,
    coef,
    flux,
    tangent,
    rhs,
    k_one,
    k_two,
    load_sem,
    knob_sems,
    xs_sems,
    xr_sems,
    ys_sems,
    yr_sems,
    fs_sems,
    fr_sems,
    rs_sems,
    rr_sems,
):
    species, reactions, groups, params, rows, x_devices, y_devices = dims
    count = params + 1
    gx, gy, me = lax.axis_index("gx"), lax.axis_index("gy"), lax.axis_index("pa")
    x_next, x_prev = lax.rem(gx + 1, x_devices), lax.rem(gx + x_devices - 1, x_devices)
    y_next, y_prev = lax.rem(gy + 1, y_devices), lax.rem(gy + y_devices - 1, y_devices)

    def peer(d):
        return lax.rem(me + d, groups)

    loads = [
        pltpu.make_async_copy(sens_hbm, sens_in, load_sem.at[0]),
        pltpu.make_async_copy(conc_hbm, conc_in, load_sem.at[1]),
        pltpu.make_async_copy(blocks_hbm, blocks_in, load_sem.at[2]),
    ]
    for load in loads:
        load.start()

    barrier = pltpu.get_barrier_semaphore()
    neighbours = [(x_prev, gy, me), (x_next, gy, me), (gx, y_prev, me), (gx, y_next, me)]
    neighbours += [(gx, gy, peer(d)) for d in range(1, groups)]
    for neighbour in neighbours:
        pl.semaphore_signal(barrier, inc=1, device_id=neighbour, device_id_type=MESH)

    lane = lax.broadcasted_iota(jnp.int32, (rows, LANES), 1)
    row = lax.broadcasted_iota(jnp.int32, (rows, LANES), 0)
    u, v, mix = u_ref[...], v_ref[...], mix_ref[...]
    u_pos, u_neg = jnp.maximum(u, 0.0), jnp.minimum(u, 0.0)
    v_pos, v_neg = jnp.maximum(v, 0.0), jnp.minimum(v, 0.0)
    from_left = jnp.where((row == 0) & (gx == 0), 0.0, u_pos + mix)
    from_right = jnp.where((row == rows - 1) & (gx == x_devices - 1), 0.0, mix - u_neg)
    from_south, from_north = v_pos + mix, mix - v_neg
    first, last = lane == 0, lane == LANES - 1
    south_edge = jnp.where(first & (gy > 0), from_south, 0.0)
    north_edge = jnp.where(last & (gy < y_devices - 1), from_north, 0.0)
    weights[0] = 1.0 - u_pos + u_neg - v_pos + v_neg - 4.0 * mix
    weights[1] = from_left
    weights[2] = from_right
    weights[3] = jnp.where(first, 0.0, from_south)
    weights[4] = jnp.where(last, 0.0, from_north)
    weights[5] = south_edge + north_edge

    tile_row = lax.broadcasted_iota(jnp.int32, (16, LANES), 0)
    tile_lane = lax.broadcasted_iota(jnp.int32, (16, LANES), 1)

    def one_hot(x, at_first, at_last):
        hit = ((tile_row == at_first + x) & (tile_lane == 0)) | (
            (tile_row == at_last + x) & (tile_lane == LANES - 1)
        )
        return jnp.where(hit, 1.0, 0.0).astype(BF16)

    gather_edge = [one_hot(x, 0, 4) for x in range(rows)]
    spread_edge = [one_hot(x, 4, 8) for x in range(rows)]

    def x_copies(sub, f):
        return [
            pltpu.make_async_remote_copy(
                src_ref=xs_send.at[sub, side, f],
                dst_ref=xs_recv.at[sub, 1 - side, f],
                send_sem=xs_sems.at[sub, side, f],
                recv_sem=xr_sems.at[sub, 1 - side, f],
                device_id=(x_prev if side == 0 else x_next, gy, me),
                device_id_type=MESH,
            )
            for side in range(2)
        ]

    def y_copies(sub, f):
        return [
            pltpu.make_async_remote_copy(
                src_ref=ys_send.at[sub, f],
                dst_ref=ys_recv.at[sub, 1 - side, f],
                send_sem=ys_sems.at[sub, side, f],
                recv_sem=yr_sems.at[sub, 1 - side, f],
                device_id=(gx, y_prev if side == 0 else y_next, me),
                device_id_type=MESH,
            )
            for side in range(2)
        ]

    def fwd_copies(c):
        return [
            pltpu.make_async_remote_copy(
                src_ref=fwd_send.at[c, peer(d)],
                dst_ref=fwd_recv.at[c, d - 1],
                send_sem=fs_sems.at[c, d - 1],
                recv_sem=fr_sems.at[c, d - 1],
                device_id=(gx, gy, peer(d)),
                device_id_type=MESH,
            )
            for d in range(1, groups)
        ]

    def ret_copies(c):
        return [
            pltpu.make_async_remote_copy(
                src_ref=ret_send.at[c, d - 1],
                dst_ref=ret_recv.at[c, d - 1],
                send_sem=rs_sems.at[c, d - 1],
                recv_sem=rr_sems.at[c, d - 1],
                device_id=(gx, gy, peer(groups - d)),
                device_id_type=MESH,
            )
            for d in range(1, groups)
        ]

    knob_copies = [
        pltpu.make_async_remote_copy(
            src_ref=knob_ref,
            dst_ref=knobs.at[d - 1],
            send_sem=knob_sems.at[0, d - 1],
            recv_sem=knob_sems.at[1, d - 1],
            device_id=(gx, gy, peer(d)),
            device_id_type=MESH,
        )
        for d in range(1, groups)
    ]

    def stage_halo(sub, f, values):
        rounded = [value.astype(BF16) for value in values]
        xs_send[sub, 0, f] = rounded[0]
        xs_send[sub, 1, f] = rounded[rows - 1]
        edge = contract(gather_edge[0], rounded[0], ((1,), (1,)))
        for x in range(1, rows):
            edge += contract(gather_edge[x], rounded[x], ((1,), (1,)))
        ys_send[sub, f, :, 0:species] = edge[0:8]

    def start_halo(sub, f):
        for copy in x_copies(sub, f) + y_copies(sub, f):
            copy.start()

    def substep(sub, f, source):
        for copy in x_copies(sub, f) + y_copies(sub, f):
            copy.wait_recv()
        beside = jnp.concatenate(
            [ys_recv[sub, 0, f, :, 0:species], ys_recv[sub, 1, f, :, 0:species]], axis=0
        ).astype(BF16)
        values = []
        for x in range(rows):
            center = source[f, x]
            left = xs_recv[sub, 0, f].astype(F32) if x == 0 else source[f, x - 1]
            right = xs_recv[sub, 1, f].astype(F32) if x == rows - 1 else source[f, x + 1]
            edge = contract(beside, spread_edge[x], ((0,), (0,)))
            w = [weights[k, x : x + 1, :] for k in range(6)]
            values.append(
                w[0] * center
                + w[1] * left
                + w[2] * right
                + w[3] * pltpu.roll(center, 1, 1)
                + w[4] * pltpu.roll(center, LANES - 1, 1)
                + w[5] * edge
            )
        return values

    def stage_input(f, held, stride, offset):
        values = []
        for x in range(rows):
            value = held[pl.ds(offset + x, species, stride=stride), :]
            fields[f, x] = value
            values.append(value)
        stage_halo(0, f, values)

    loads[0].wait()
    loads[1].wait()
    stage_input(params, conc_in, rows, 0)
    pl.semaphore_wait(barrier, len(neighbours))
    for copy in knob_copies:
        copy.start()

    @pl.loop(0, params)
    def _(f):
        stage_input(f, sens_in, params * rows, f * rows)
        start_halo(0, f)

    start_halo(0, params)

    def relayout(begin, end):
        @pl.loop(begin, end)
        def _(i):
            solver[pl.ds(i, species, stride=species), :] = blocks_in[i].astype(F32)

    loads[2].wait()
    relayout(0, species // 2)

    @pl.loop(0, count)
    def _(f):
        values = substep(0, f, fields)
        for x in range(rows):
            stepped[f, x] = values[x]
        stage_halo(1, f, values)
        start_halo(1, f)

    relayout(species // 2, species)

    @pl.loop(0, params)
    def _(f):
        values = substep(1, f, stepped)
        for x in range(rows):
            fields[f, x] = values[x]
            fwd_send[f, x] = values[x].astype(BF16)
        for copy in fwd_copies(f):
            copy.start()

    values = substep(1, params, stepped)
    for x in range(rows):
        fields[params, x] = values[x]

    conc = fields[params, me]
    conc_hi = conc.astype(BF16)
    conc_lo = (conc - conc_hi.astype(F32)).astype(BF16)
    inverse_temp = 1.0 / temp_ref[pl.ds(me, 1), :] - 1.0 / 298.0
    rate = rate_ref[0] * jnp.exp(-rate_ref[1] * inverse_temp)
    for side in range(2):
        pick = pick_ref[(1 - side) * reactions : (2 - side) * reactions, :]
        reactant = contract(pick, conc_hi, ((1,), (0,))) + contract(pick, conc_lo, ((1,), (0,)))
        coef[side] = (rate * reactant).astype(BF16).astype(F32)

    ground = ground_ref[pl.ds(me, 1), :]
    zone = zone_ref[pl.ds(me, 1), :]
    species_ids = lax.broadcasted_iota(jnp.int32, (species, LANES), 0)
    for copy in knob_copies:
        copy.wait_recv()

    def source(c, d):
        held = knob_ref if d == 0 else knobs.at[d - 1]
        hit = (species_ids == held[pl.ds(c, 1), :]) & (zone == held[pl.ds(params + c, 1), :])
        return jnp.where(hit, ground, 0.0)

    step = 128
    blocks_of_reactions = [(b, min(b + step, reactions)) for b in range(0, reactions, step)]

    def jacobian(v_bf):
        for begin, end in blocks_of_reactions:
            left = contract(pick_ref[begin:end, :], v_bf, ((1,), (0,)))
            right = contract(pick_ref[reactions + begin : reactions + end, :], v_bf, ((1,), (0,)))
            for d in range(groups):
                at = slice(d * LANES, (d + 1) * LANES)
                flux[begin:end, at] = (
                    coef[0, begin:end, :] * left[:, at] + coef[1, begin:end, :] * right[:, at]
                ).astype(BF16)
        return contract(net_ref[...], flux[...], ((1,), (0,)))

    width = 40 if species % 40 == 0 else 8

    def solve(result):
        for begin in range(0, species, width):

            def body(j, sums):
                block = solver[pl.ds(j * species + begin, width), :]
                return tuple(sums[d] + block * rhs[d, pl.ds(j, 1), :] for d in range(groups))

            zero = jnp.zeros((width, LANES), F32)
            sums = lax.fori_loop(0, species, body, (zero,) * groups, unroll=4)
            for d in range(groups):
                result[d, begin : begin + width, :] = sums[d]

    @pl.loop(0, params)
    def _(c):
        for copy in fwd_copies(c):
            copy.wait_recv()
        tiles = [fwd_send[c, me]] + [fwd_recv[c, d - 1] for d in range(1, groups)]
        tangent[...] = jnp.concatenate(tiles, axis=1)
        product = jacobian(tangent[...])
        for d in range(groups):
            rhs[d] = product[:, d * LANES : (d + 1) * LANES] + source(c, d)
        solve(k_one)
        for d in range(groups):
            at = slice(d * LANES, (d + 1) * LANES)
            tangent[:, at] = (tangent[:, at].astype(F32) + k_one[d]).astype(BF16)
        product = jacobian(tangent[...])
        for d in range(groups):
            rhs[d] = product[:, d * LANES : (d + 1) * LANES] + source(c, d) - 2.0 * k_one[d]
        solve(k_two)
        for d in range(1, groups):
            ret_send[c, d - 1] = (1.5 * k_one[d] + 0.5 * k_two[d]).astype(BF16)
        for copy in ret_copies(c):
            copy.start()
        out_ref[c, me] = fields[c, me] + 1.5 * k_one[0] + 0.5 * k_two[0]

    @pl.loop(0, params)
    def _(c):
        for copy in ret_copies(c):
            copy.wait_recv()
        for d in range(1, groups):
            x = peer(d)
            out_ref[c, x] = fields[c, x] + ret_recv[c, d - 1].astype(F32)

    for copy in knob_copies:
        copy.wait_send()

    @pl.loop(0, count)
    def _(f):
        for sub in range(NSUB):
            for copy in x_copies(sub, f) + y_copies(sub, f):
                copy.wait_send()

    @pl.loop(0, params)
    def _(c):
        for copy in fwd_copies(c) + ret_copies(c):
            copy.wait_send()


def shards(
    mixing_ratios,
    derivative_field,
    thermal_kelvin,
    eastward_cfl_ratio,
    northward_cfl_ratio,
    lateral_mixing_coef,
    prefactor_times_dt,
    barrier_kelvin,
    input_compound_pair,
    output_yield_matrix,
    partition_solver_matrices,
    ground_flux_per_tick,
    cell_zone_label,
    knob_target_compound,
    knob_zone,
):
    species, params, _, rows, lanes = derivative_field.shape
    reactions = prefactor_times_dt.shape[0]
    groups = lax.axis_size("pa")
    x_devices, y_devices = lax.axis_size("gx"), lax.axis_size("gy")
    count = params + 1

    species_ids = jnp.arange(species, dtype=jnp.int32)
    hit = input_compound_pair.T.reshape(-1)[:, None] == species_ids[None, :]
    pick = hit.astype(BF16)
    consumed = (species_ids[:, None] == input_compound_pair[None, :, 0]).astype(jnp.int32) + (
        species_ids[:, None] == input_compound_pair[None, :, 1]
    ).astype(jnp.int32)
    net = (output_yield_matrix - consumed).astype(BF16)
    rates = jnp.broadcast_to(
        jnp.stack([prefactor_times_dt, barrier_kelvin])[:, :, None], (2, reactions, lanes)
    )
    knob = jnp.broadcast_to(
        jnp.concatenate([knob_target_compound, knob_zone])[:, None], (2 * params, lanes)
    )

    vmem = pl.BlockSpec(memory_space=pltpu.VMEM)
    hbm = pl.BlockSpec(memory_space=pl.ANY)
    dma = pltpu.SemaphoreType.DMA
    tile = (species, lanes)
    moved = pl.pallas_call(
        functools.partial(
            kernel, (species, reactions, groups, params, rows, x_devices, y_devices)
        ),
        out_shape=jax.ShapeDtypeStruct((params, rows, species, lanes), F32),
        in_specs=[hbm] * 3 + [vmem] * 10,
        out_specs=vmem,
        scratch_shapes=[
            pltpu.VMEM((species * params * rows, lanes), F32),
            pltpu.VMEM((species * rows, lanes), F32),
            pltpu.VMEM((species, species, lanes), BF16),
            pltpu.VMEM((species * species, lanes), F32),
            pltpu.VMEM((count, rows) + tile, F32),
            pltpu.VMEM((count, rows) + tile, F32),
            pltpu.VMEM((6, rows, lanes), F32),
            pltpu.VMEM((NSUB, 2, count) + tile, BF16),
            pltpu.VMEM((NSUB, 2, count) + tile, BF16),
            pltpu.VMEM((NSUB, count, 8, lanes), F32),
            pltpu.VMEM((NSUB, 2, count, 8, lanes), F32),
            pltpu.VMEM((params, rows) + tile, BF16),
            pltpu.VMEM((params, groups - 1) + tile, BF16),
            pltpu.VMEM((params, groups - 1) + tile, BF16),
            pltpu.VMEM((params, groups - 1) + tile, BF16),
            pltpu.VMEM((groups - 1, 2 * params, lanes), jnp.int32),
            pltpu.VMEM((2, reactions, lanes), F32),
            pltpu.VMEM((reactions, groups * lanes), BF16),
            pltpu.VMEM((species, groups * lanes), BF16),
            pltpu.VMEM((groups,) + tile, F32),
            pltpu.VMEM((groups,) + tile, F32),
            pltpu.VMEM((groups,) + tile, F32),
            dma((3,)),
            dma((2, groups - 1)),
            dma((NSUB, 2, count)),
            dma((NSUB, 2, count)),
            dma((NSUB, 2, count)),
            dma((NSUB, 2, count)),
            dma((params, groups - 1)),
            dma((params, groups - 1)),
            dma((params, groups - 1)),
            dma((params, groups - 1)),
        ],
        compiler_params=pltpu.CompilerParams(
            collective_id=0, has_side_effects=True, vmem_limit_bytes=40 * 2**20
        ),
        name="sensitivity_step",
    )(
        derivative_field.reshape(species * params * rows, lanes),
        mixing_ratios.reshape(species * rows, lanes),
        partition_solver_matrices.reshape(species, species, lanes),
        thermal_kelvin.reshape(rows, lanes),
        eastward_cfl_ratio.reshape(rows, lanes),
        northward_cfl_ratio.reshape(rows, lanes),
        lateral_mixing_coef.reshape(rows, lanes),
        ground_flux_per_tick,
        cell_zone_label,
        knob,
        rates,
        pick,
        net,
    )
    return jnp.transpose(moved, (2, 0, 1, 3))[:, :, None]


def solution(mesh):
    in_specs = (
        P(None, None, "gx", "gy"),
        P(None, "pa", None, "gx", "gy"),
        P(None, "gx", "gy"),
        P(None, "gx", "gy"),
        P(None, "gx", "gy"),
        P(None, "gx", "gy"),
        P(),
        P(),
        P(),
        P(),
        P(None, None, None, ("gx", "pa"), "gy"),
        P("gx", "gy"),
        P("gx", "gy"),
        P("pa"),
        P("pa"),
    )
    out_specs = P(None, "pa", None, "gx", "gy")
    return jax.shard_map(shards, mesh=mesh, in_specs=in_specs, out_specs=out_specs, check_vma=False)
```
